256 devices in a mesh: dp: 16 (over z, core), seq: 4 (over y), vocab: 4 (over x).
Axes of the slice: x: 4, y: 4, z: 8, core: 2. Of those that a mesh axis runs over, the one named last changes fastest.
Arguments:
- hidden: bfloat16 [1024, 4096], P(('dp', 'vocab'), 'seq'), may hold values from -40 to 40
- head_weight: bfloat16 [4096, 81920], P('seq', ('dp', 'vocab')), may hold values from -1 to 1
- targets: int32 [1024], replicated, may hold values from 0 to 81919
- weights: float32 [1024], replicated, may hold values from -4 to 4
Outputs:
- log_prob: float32 [1024], P('seq')
- hidden_grad: bfloat16 [1024, 4096], P(('dp', 'vocab'), 'seq')
- head_grad: bfloat16 [4096, 81920], P('seq', ('dp', 'vocab'))
The draws below stay inside these ranges and needn't reach their ends.
All inputs are finite; a program needn't handle non-finite values.
Results may differ from the reference program's by a relative error of at most 0.0047.
Values may be sent and summed in bfloat16 or wider, within the bound.
No kernel may reach another device: no remote copies, remote signals or barrier semaphores. Data moves between devices by JAX's collectives and lax.ppermute only.
A program may use at most 64 MiB of HBM per device.

```python
import math
import jax
import jax.numpy as jnp
import numpy as np
from jax import lax

D = 4096
VOC_DEV = 1280
VOCAB = 81920
TOKENS = 1024


def draw_hidden(key, part):
    key = jax.random.fold_in(key, 1)
    first_key = jax.random.fold_in(key, 0)
    base_rows = jnp.clip(jax.random.normal(first_key, (TOKENS, D), jnp.float32), -6.0, 6.0)
    return base_rows.astype(jnp.bfloat16)


def draw_head_weight(key, part):
    key = jax.random.fold_in(key, 2)
    rest = jnp.clip(jax.random.normal(key, (D, VOCAB), jnp.float32), -6.0, 6.0) * (3.0 / math.sqrt(D))
    return jnp.clip(rest, -1.0, 1.0).astype(jnp.bfloat16)


def plant(result, stream_key, least, top_value):
    longest = result.shape.index(max(result.shape))
    spots = []
    for shift in (0, 1):
        where = [jax.random.randint(jax.random.fold_in(stream_key, axis), (), 0, length) for axis, length in enumerate(result.shape)]
        where[longest] = (where[longest] + shift) % result.shape[longest]
        spots.append(tuple(where))
    return result.at[spots[0]].set(least).at[spots[1]].set(top_value)


def skewed_wide(own_key, extent, amount, skew):
    loads = [min(1 << octave, amount + 1 - (1 << octave)) * (1 << 20) // math.isqrt((1 << octave) ** skew) + 1 for octave in range((amount + 1).bit_length()) if 1 << octave <= amount]
    deviation = 1 + sum(loads) // (1 << 30)
    grid = np.cumsum(np.array([max(1, weight // deviation) for weight in loads]))
    ticket = jax.random.randint(jax.random.fold_in(own_key, 1), extent, 0, int(grid[len(loads) - 1]))
    start = jnp.left_shift(1, jnp.searchsorted(jnp.asarray(grid, jnp.int32), ticket, side="right").astype(jnp.int32))
    standing = start - 1 + jax.random.randint(jax.random.fold_in(own_key, 4), extent, 0, 1 << 30) % jnp.minimum(start, amount + 1 - start)
    return jax.random.permutation(jax.random.fold_in(own_key, 2), amount)[standing].astype(jnp.int32)


def bell_draw(stream_key, dims, width, most, kind=jnp.bfloat16):
    drawn = width * jax.random.normal(stream_key, dims, jnp.float32)
    return jnp.clip(drawn, min=-most, max=most).astype(kind)


def setup_inputs(seed: int = 0) -> dict:
    seeds = jax.random.split(jax.random.key(seed), 5)
    return {
        "hidden": draw_hidden(jax.random.fold_in(seeds[4], 71), 0),
        "head_weight": draw_head_weight(jax.random.fold_in(seeds[4], 71), 0),
        "targets": plant(skewed_wide(seeds[2], (TOKENS,), VOCAB, 2), jax.random.fold_in(seeds[2], 3), 0, VOCAB - 1).astype(jnp.int32),
        "weights": bell_draw(seeds[3], (TOKENS,), 1.0, 4.0, jnp.float32),
    }


def reference(hidden, head_weight, targets, weights):
    logits = jnp.dot(hidden, head_weight, preferred_element_type=jnp.float32)
    row_max = jnp.max(logits, axis=1)
    sum_total = jnp.sum(jnp.exp(logits - row_max[:, None]), axis=1)
    log_total = row_max + jnp.log(sum_total)
    column_ids = jnp.arange(VOCAB, dtype=jnp.int32)
    is_target = column_ids[None, :] == targets.astype(jnp.int32)[:, None]
    picked = jnp.sum(jnp.where(is_target, logits, jnp.zeros_like(logits)), axis=1)
    log_prob = picked - log_total
    softmax_rows = jnp.exp(logits - log_total[:, None])
    logit_grad = (weights[:, None] * (is_target.astype(jnp.float32) - softmax_rows)).astype(jnp.bfloat16)
    hidden_grad = jnp.dot(logit_grad, head_weight.T, preferred_element_type=jnp.float32).astype(jnp.bfloat16)
    grad_blocks = logit_grad.reshape(TOKENS, VOCAB // VOC_DEV, VOC_DEV).transpose(1, 0, 2)

    def one_block(piece):
        return jnp.dot(hidden.T, piece, preferred_element_type=jnp.float32).astype(jnp.bfloat16)

    head_grad = lax.map(one_block, grad_blocks).transpose(1, 0, 2).reshape(D, VOCAB)
    return (log_prob, hidden_grad, head_grad)
```

```python
import jax
import jax.numpy as jnp
from jax import lax
from jax.sharding import Mesh, PartitionSpec as P

F32 = jnp.float32
BF16 = jnp.bfloat16
NZ, NC, NY, NX = 8, 2, 4, 4


def shift(n, d):
    return [(i, (i + d) % n) for i in range(n)]


def merge(stats):
    m = jnp.max(stats[:, 0], axis=0)
    s = jnp.sum(stats[:, 1] * jnp.exp(stats[:, 0] - m[None]), axis=0)
    return jnp.stack([m, s, jnp.sum(stats[:, 2], axis=0)])


def spread(stats, axes, n):
    flat = jnp.broadcast_to(stats.reshape(1, 12, 128), (n, 12, 128))
    flat = jnp.pad(flat, ((0, 0), (0, 4), (0, 0))).reshape(n * 16, 128)
    got = lax.all_to_all(flat, axes, 0, 0, tiled=True)
    return got.reshape(n, 16, 128)[:, :12].reshape(n, 3, 4, 128)


def body(hidden, head, targets, weights):
    rows, width = hidden.shape
    columns = head.shape[1]
    z, c, y, x = (lax.axis_index(a) for a in ("z", "core", "y", "x"))
    swap = [(0, 1), (1, 0)]
    group = NC * columns // NY
    tokens = NZ * NX * rows

    copies = jnp.broadcast_to(hidden[None], (NY * NX, rows, width)).reshape(NY * NX * rows, width)
    near = lax.all_to_all(copies, ("y", "x"), 0, 0, tiled=True)
    near = near.reshape(NY, NX, rows, width).transpose(1, 2, 0, 3).reshape(NX * rows, NY * width)
    half = NY * width // 2
    parts = (near[:, :half], near[:, half:])
    full = jnp.zeros((NZ, NX * rows, NY * width), BF16)
    full = lax.dynamic_update_slice(full, near[None], (z, 0, 0))
    flying = {(p, d): parts[p] for p in (0, 1) for d in (1, -1)}
    for step in range(1, 5):
        for p in (0, 1):
            for d in (1, -1):
                if step == 4 and d == (1, -1)[p]:
                    continue
                flying[p, d] = lax.ppermute(flying[p, d], "z", shift(NZ, d))
                full = lax.dynamic_update_slice(
                    full, flying[p, d][None], ((z - d * step) % NZ, 0, p * half)
                )
    hid = full.reshape(tokens, NY * width)

    other = lax.ppermute(head, "core", swap)
    both = jnp.where(c == 0, jnp.stack([head, other]), jnp.stack([other, head]))
    chip_head = both.transpose(1, 0, 2).reshape(width, NC * columns)
    half_rows = width // NC
    mine = lax.dynamic_slice_in_dim(chip_head, c * half_rows, half_rows, 0)
    blocks = jnp.zeros((NY, NC, half_rows, group), BF16)
    for d in range(NY):
        block = lax.dynamic_slice_in_dim(mine, ((y + d) % NY) * group, group, 1)
        if d:
            block = lax.ppermute(block, "y", shift(NY, d))
        twin = lax.ppermute(block, "core", swap)
        origin = (y - d) % NY
        blocks = lax.dynamic_update_slice(blocks, block[None, None], (origin, c, 0, 0))
        blocks = lax.dynamic_update_slice(blocks, twin[None, None], (origin, 1 - c, 0, 0))
    head_group = blocks.reshape(NY * width, group)

    logits = jnp.dot(hid, head_group, preferred_element_type=F32)
    grid = lambda v: lax.dynamic_index_in_dim(v.reshape(NZ, NC, NX * rows), c, 1, False).reshape(tokens)
    my_targets, my_weights = grid(targets), grid(weights)
    pair = lax.axis_index(("z", "core", "x")) - c * NX
    lanes = jnp.arange(NC * columns, dtype=jnp.int32)
    ids = (pair + NX * (lanes // columns)) * columns + lanes % columns
    ids_here = lax.dynamic_slice_in_dim(ids, y * group, group, 0)
    row_max = jnp.max(logits, axis=1)
    e = jnp.exp(logits - row_max[:, None])
    row_sum = jnp.sum(e, axis=1)
    picked = jnp.sum(jnp.where(ids_here[None, :] == my_targets[:, None], logits, 0.0), axis=1)
    e = e.astype(BF16)

    e_full = jnp.zeros((tokens, NC * columns), BF16)
    for d in (0, 1, 3, 2):
        got = lax.ppermute(e, "y", shift(NY, d)) if d else e
        e_full = lax.dynamic_update_slice(e_full, got, (0, ((y - d) % NY) * group))

    stats = jnp.stack([row_max, row_sum, picked]).reshape(3, 4, 128)
    close = spread(stats, ("y", "x"), NY * NX)
    maxes = lax.dynamic_index_in_dim(close[:, 0].reshape(NY, NX, tokens), x, 1, False)
    stats = merge(spread(merge(close), ("z",), NZ)).reshape(3, tokens)
    log_total = stats[0] + jnp.log(stats[1])
    log_prob = stats[2] - log_total
    scale = -my_weights[None] * jnp.exp(maxes - log_total[None])
    target_grad = my_weights * (1.0 - jnp.exp(log_prob))

    own = lax.dynamic_slice_in_dim(log_prob, y * (tokens // NY), tokens // NY, 0)
    oth = lax.ppermute(own, "core", swap)
    pairs = jnp.where(c == 0, jnp.stack([own, oth]), jnp.stack([oth, own]))
    log_prob_out = pairs.reshape(NC, 2, NX * rows).transpose(1, 0, 2).reshape(-1)

    scales = jnp.concatenate(
        [jnp.broadcast_to(scale[g][:, None], (tokens, group)) for g in range(NY)], axis=1
    )
    grad = jnp.where(
        ids[None, :] == my_targets[:, None], target_grad[:, None], e_full.astype(F32) * scales
    ).astype(BF16)

    part = lax.dot_general(grad, chip_head, (((1,), (1,)), ((), ())), preferred_element_type=F32)
    part = part.reshape(NZ, NX, rows, width)
    total = lax.dynamic_index_in_dim(part, x, 1, False)
    for d in (2, 1, 3):
        send = lax.dynamic_index_in_dim(part, (x + d) % NX, 1, False).astype(BF16)
        total = total + lax.ppermute(send, "x", shift(NX, d)).astype(F32)
    got = lax.all_to_all(total.reshape(NZ * rows, width), "z", 0, 0, tiled=True)
    hidden_grad = jnp.sum(got.reshape(NZ, rows, width), axis=0).astype(BF16)

    my_cols = lax.dynamic_slice_in_dim(grad, c * columns, columns, 1)
    twin_cols = lax.ppermute(
        lax.dynamic_slice_in_dim(grad, (1 - c) * columns, columns, 1), "core", swap
    )
    my_slice = lax.dynamic_slice_in_dim(hid, y * width, width, 1)
    twin_slice = lax.ppermute(my_slice, "core", swap)
    contract = (((0,), (0,)), ((), ()))
    head_grad = (
        lax.dot_general(my_slice, my_cols, contract, preferred_element_type=F32)
        + lax.dot_general(twin_slice, twin_cols, contract, preferred_element_type=F32)
    ).astype(BF16)
    return log_prob_out, hidden_grad, head_grad


def solution(mesh):
    fine = Mesh(mesh.devices.reshape(NZ, NC, NY, NX), ("z", "core", "y", "x"))
    tok = ("z", "core", "x")
    return jax.shard_map(
        body,
        mesh=fine,
        in_specs=(P(tok, "y"), P("y", tok), P(), P()),
        out_specs=(P("y"), P(tok, "y"), P("y", tok)),
        check_vma=False,
    )
```

```python
import jax
import jax.numpy as jnp
from jax import lax
from jax.experimental import pallas as pl
from jax.experimental.pallas import tpu as pltpu
from jax.sharding import Mesh, PartitionSpec as P

F32 = jnp.float32
BF16 = jnp.bfloat16
NZ, NC, NY, NX = 8, 2, 4, 4
VMEM = pl.BlockSpec(memory_space=pltpu.VMEM)
SMEM = pl.BlockSpec(memory_space=pltpu.SMEM)


def shift(n, d):
    return [(i, (i + d) % n) for i in range(n)]


SWAP = [(0, 1), (1, 0)]


ANY = pl.BlockSpec(memory_space=pl.ANY)


def call(kernel, outs, args, scratch=(), flops=1000, moved=1000, far=0):
    return pl.pallas_call(
        kernel,
        out_shape=[jax.ShapeDtypeStruct(s, d) for s, d in outs],
        in_specs=[SMEM] + [VMEM] * (len(args) - 1 - far) + [ANY] * far,
        out_specs=[VMEM] * len(outs),
        scratch_shapes=list(scratch),
        cost_estimate=pl.CostEstimate(flops=flops, bytes_accessed=moved, transcendentals=0),
        compiler_params=pltpu.CompilerParams(vmem_limit_bytes=24 * 2**20),
    )(*args)


def logits_kernel(pos, targets, b0, b1, b2, b3, hid, *refs):
    e_out, stats_out, slice_out, acc, hid_v, sems = refs
    z, c, y, x = (pos[i] for i in range(4))
    width, group = b0.shape
    rows = e_out.shape[0]
    copies = []
    for i in range(4):
        core = c if i < 2 else 1 - c
        origin = 2 * core + lax.rem(y + i, 2)
        cols = pl.ds(pl.multiple_of(origin * width, 128), width)
        copies.append(pltpu.make_async_copy(hid.at[:, cols], hid_v.at[i], sems.at[i]))
    for copy in copies:
        copy.start()
    for i, block in enumerate((b0, b1, b2, b3)):
        copies[i].wait()
        term = jnp.dot(hid_v[i], block[...], preferred_element_type=F32)
        acc[...] = term if i == 0 else acc[...] + term

        @pl.when((c if i < 2 else 1 - c) * 2 + lax.rem(y + i, 2) == y)
        def _():
            slice_out[...] = hid_v[i]

    logits = acc[...]
    top = jnp.max(logits, axis=1, keepdims=True)
    e = jnp.exp(logits - top)
    total = jnp.sum(e, axis=1, keepdims=True)
    first = ((z * NC + y // 2) * NX + x) * (2 * group) + lax.rem(y, 2) * group
    ids = first + lax.broadcasted_iota(jnp.int32, (rows, group), 1)
    picked = jnp.sum(jnp.where(ids == targets[...], logits, 0.0), axis=1, keepdims=True)
    e_out[...] = e.astype(BF16)
    lane = lax.broadcasted_iota(jnp.int32, (rows, 128), 1)
    table = jnp.where(lane == 0, top, jnp.where(lane == 1, total, jnp.where(lane == 2, picked, 0.0)))
    flat = table.T
    packed = pack([flat[0:1], flat[1:2], flat[2:3]])
    for i in range(stats_out.shape[0]):
        stats_out[i] = packed


def pack(vectors):
    parts = [v[:, i : i + 128] for v in vectors for i in range(0, v.shape[1], 128)]
    return jnp.concatenate(parts + [jnp.zeros((16 - len(parts), 128), F32)], axis=0)


def unpack(tiles):
    return jnp.concatenate([tiles[i : i + 1] for i in range(tiles.shape[0])], axis=1)


def merged(table):
    m, s, p = table[:, 0:4], table[:, 4:8], table[:, 8:12]
    top = jnp.max(m, axis=0)
    return top, jnp.sum(s * jnp.exp(m - top[None]), axis=0), jnp.sum(p, axis=0)


def near_kernel(pos, got, out):
    m, s, p = merged(got[...])
    packed = jnp.concatenate([m, s, p, jnp.zeros_like(m)], axis=0)
    for i in range(out.shape[0]):
        out[i] = packed


def far_kernel(pos, far, near, weights, vec_out, log_prob_out):
    y = pos[2]
    m, s, p = (unpack(v) for v in merged(far[...]))
    log_total = m + jnp.log(s)
    log_prob = p - log_total
    w = weights[...]
    rows = []
    for d in range(NY):
        local = unpack(near[lax.rem(y + NY - d, NY)][0:4])
        rows.append(-w * jnp.exp(local - log_total))
    rows.append(w * (1.0 - jnp.exp(log_prob)))
    rows.append(jnp.zeros((3, m.shape[1]), F32))
    vec_out[...] = jnp.concatenate(rows, axis=0)
    log_prob_out[...] = jnp.broadcast_to(log_prob, log_prob_out.shape)


def grad_kernel(pos, targets, vec, e0, e1, e2, e3, own, other, g0, g1, keep, s1, s2, s3, part):
    z, c, y, x = (pos[i] for i in range(4))
    rows, group = e0.shape
    cols = jnp.concatenate([vec[...], jnp.zeros((120, rows), F32)], axis=0).T
    t = targets[...]
    for d, e in enumerate((e0, e1, e2, e3)):
        g = lax.rem(y + NY - d, NY)
        first = ((z * NC + g // 2) * NX + x) * (2 * group) + lax.rem(g, 2) * group
        ids = first + lax.broadcasted_iota(jnp.int32, (rows, group), 1)
        value = jnp.where(ids == t, cols[:, 4:5], e[...].astype(F32) * cols[:, d : d + 1])
        value = value.astype(BF16)
        at = pl.ds(pl.multiple_of(lax.rem(g, 2) * group, 128), group)
        same = g // 2 == c

        @pl.when(same)
        def _():
            g0[:, at] = value

        @pl.when(jnp.logical_not(same))
        def _():
            g1[:, at] = value

    nt = (((1,), (1,)), ((), ()))
    sums = lax.dot_general(g0[...], own[...], nt, preferred_element_type=F32)
    sums += lax.dot_general(g1[...], other[...], nt, preferred_element_type=F32)
    part[...] = sums.reshape(part.shape)
    keep[...] = part[:, x]
    for d, out in enumerate((s1, s2, s3)):
        out[...] = part[:, lax.rem(x + d + 1, NX)].astype(BF16)


def head_kernel(pos, h0, h1, g0, g1, out):
    tn = (((0,), (0,)), ((), ()))
    step = 256
    for i in range(0, out.shape[0], step):
        total = lax.dot_general(h0[:, i : i + step], g0[...], tn, preferred_element_type=F32)
        total += lax.dot_general(h1[:, i : i + step], g1[...], tn, preferred_element_type=F32)
        out[i : i + step] = total.astype(BF16)


def tie(*arrays):
    return lax.optimization_barrier(arrays)


def body(hidden, head, targets, weights):
    rows, width = hidden.shape
    columns = head.shape[1]
    group = columns // 2
    half = width // 2
    per_z = NX * rows
    z, c, y, x = (lax.axis_index(a) for a in ("z", "core", "y", "x"))
    pos = jnp.stack([z, c, y, x]).astype(jnp.int32)

    def copies(v, n, axis):
        flat = jnp.broadcast_to(v[None], (n,) + v.shape).reshape((n * v.shape[0],) + v.shape[1:])
        return lax.all_to_all(flat, axis, 0, 0, tiled=True).reshape((n,) + v.shape)

    near = copies(hidden, NY, "y")
    def block(k):
        return lax.dynamic_slice_in_dim(head, ((y + k) % 2) * group, group, 1)

    def hand_over(v, k):
        perm = [
            (i * NY + j, (j // 2) * NY + 2 * i + (j + k) % 2) for i in range(NC) for j in range(NY)
        ]
        return lax.ppermute(v, ("core", "y"), perm)

    near, block0, block1 = tie(near, block(0), block(1))
    got0, got1 = hand_over(block0, 0), hand_over(block1, 1)
    near = near.transpose(1, 0, 2).reshape(rows, NY * width)
    near = copies(near, NX, "x").reshape(per_z, NY * width)

    def ordered(v):
        v = lax.dynamic_index_in_dim(v.reshape(NZ, NC, per_z), c, 1, False)
        return v.reshape(NZ * per_z)

    my_targets, my_weights = ordered(targets)[:, None], ordered(weights)[None]

    hid = lax.all_gather(near, "z", axis=0, tiled=True)
    twin0, twin1 = lax.ppermute(got0, "core", SWAP), lax.ppermute(got1, "core", SWAP)
    twin0, twin1, head_later = tie(twin0, twin1, head)
    other = lax.ppermute(head_later, "core", SWAP)

    size = NZ * per_z
    e, stats, mine = call(
        logits_kernel,
        [((size, group), BF16), ((NY, 16, 128), F32), ((size, width), BF16)],
        (pos, my_targets, got0, got1, twin0, twin1, hid),
        scratch=[
            pltpu.VMEM((size, group), F32),
            pltpu.VMEM((NY, size, width), BF16),
            pltpu.SemaphoreType.DMA((NY,)),
        ],
        far=1,
    )

    close = lax.all_to_all(stats, "y", 0, 0, tiled=True)
    close, e, mine = tie(close, e, mine)
    exps = [e] + [lax.ppermute(e, "y", shift(NY, d)) for d in (2, 1, 3)]
    exps = [exps[0], exps[2], exps[1], exps[3]]
    (wide,) = call(near_kernel, [((NZ * NX, 16, 128), F32)], (pos, close))
    far = lax.all_to_all(wide, ("z", "x"), 0, 0, tiled=True)
    vec, lp = call(
        far_kernel, [((8, size), F32), ((8, size), F32)], (pos, far, close, my_weights)
    )
    twin_mine = lax.ppermute(mine, "core", SWAP)

    kept, sent, keep, *send = call(
        grad_kernel,
        [((size, columns), BF16)] * 2
        + [((NZ, rows, width), F32)]
        + [((NZ, rows, width), BF16)] * 3,
        (pos, my_targets, vec, *exps, head, other),
        scratch=[pltpu.VMEM((NZ, NX, rows, width), F32)],
    )
    for d, v in enumerate(send):
        keep = keep + lax.ppermute(v, "x", shift(NX, d + 1)).astype(F32)
    twin_kept = lax.ppermute(sent, "core", SWAP)
    keep, twin_kept, twin_mine = tie(keep, twin_kept, twin_mine)

    total = keep.astype(BF16).reshape(NZ * rows, width)
    got = lax.all_to_all(total, "z", 0, 0, tiled=True)
    (head_grad,) = call(
        head_kernel,
        [((width, columns), BF16)],
        (pos, mine, twin_mine, kept, twin_kept),
        flops=2 * NZ * NC * per_z * columns * width,
        moved=8 * 2**20,
    )
    hidden_grad = jnp.sum(got.reshape(NZ, rows, width).astype(F32), axis=0).astype(BF16)

    log_prob = lp[0]
    own = lax.dynamic_slice_in_dim(log_prob, 2 * y * per_z, 2 * per_z, 0)
    oth = lax.ppermute(own, "core", SWAP)
    pairs = jnp.where(c == 0, jnp.stack([own, oth]), jnp.stack([oth, own]))
    log_prob_out = pairs.reshape(NC, 2, per_z).transpose(1, 0, 2).reshape(-1)
    return log_prob_out, hidden_grad, head_grad


def solution(mesh):
    fine = Mesh(mesh.devices.reshape(NZ, NC, NY, NX), ("z", "core", "y", "x"))
    tok = ("z", "core", "x")
    return jax.shard_map(
        body,
        mesh=fine,
        in_specs=(P(tok, "y"), P("y", tok), P(), P()),
        out_specs=(P("y"), P(tok, "y"), P("y", tok)),
        check_vma=False,
    )
```

```python
import functools

import jax
import jax.numpy as jnp
from jax import lax
from jax.experimental import pallas as pl
from jax.experimental.pallas import tpu as pltpu
from jax.sharding import Mesh, PartitionSpec as P

F32 = jnp.float32
BF16 = jnp.bfloat16
NZ, NC, NY, NX = 8, 2, 4, 4
VMEM = pl.BlockSpec(memory_space=pltpu.VMEM)
SMEM = pl.BlockSpec(memory_space=pltpu.SMEM)


def shift(n, d):
    return [(i, (i + d) % n) for i in range(n)]


SWAP = [(0, 1), (1, 0)]


ANY = pl.BlockSpec(memory_space=pl.ANY)


def call(kernel, outs, args, scratch=(), flops=1000, moved=1000, far=0, vmem=24):
    return pl.pallas_call(
        kernel,
        out_shape=[jax.ShapeDtypeStruct(s, d) for s, d in outs],
        in_specs=[SMEM] + [VMEM] * (len(args) - 1 - far) + [ANY] * far,
        out_specs=[VMEM] * len(outs),
        scratch_shapes=list(scratch),
        cost_estimate=pl.CostEstimate(flops=flops, bytes_accessed=moved, transcendentals=0),
        compiler_params=pltpu.CompilerParams(vmem_limit_bytes=vmem * 2**20),
    )(*args)


def early_kernel(count, pos, targets, *refs):
    pieces, blocks = refs[:count], refs[count : count + 4]
    e_out, table_out, slice_out, acc, hid_v, block_v, hid_sem, block_sem = refs[count + 4 :]
    z, c, y, x = (pos[i] for i in range(4))
    _, width, group = block_v.shape
    per_z = pieces[0].shape[0]
    block_copies = [
        pltpu.make_async_copy(b, block_v.at[i], block_sem.at[i]) for i, b in enumerate(blocks)
    ]
    copies = []
    for i, p in enumerate(pieces):
        first = lax.rem(z + i + 3 * (i > 2), NZ) * per_z
        at = pl.ds(pl.multiple_of(first, 64), per_z)
        copies.append(pltpu.make_async_copy(p, hid_v.at[at], hid_sem.at[i]))
    for copy in copies + block_copies:
        copy.start()
    for ahead in (3, 4, 5):
        hid_v[pl.ds(pl.multiple_of(lax.rem(z + ahead, NZ) * per_z, 64), per_z)] = jnp.zeros(
            (per_z, hid_v.shape[1]), BF16
        )
    for copy in copies:
        copy.wait()
    multiply(hid_v, block_v, block_copies, acc, c, y)
    slice_out[...] = columns(hid_v, y, width)
    e_out[...], table_out[...] = soften(acc[...], targets[...], z, y, x)


def late_kernel(pos, targets, e_in, table_in, slice_in, p3, p5, p4a, p4b, b0, b1, b2, b3, *refs):
    e_out, slice_out, stats_out, table, acc, hid_v, block_v, hid_sem, block_sem = refs
    z, c, y, x = (pos[i] for i in range(4))
    _, width, group = block_v.shape
    per_z = p3.shape[0]
    block_copies = [
        pltpu.make_async_copy(b, block_v.at[i], block_sem.at[i])
        for i, b in enumerate((b0, b1, b2, b3))
    ]
    copies = [
        pltpu.make_async_copy(p, hid_v.at[pl.ds(first, p.shape[0])], hid_sem.at[i])
        for i, (p, first) in enumerate(
            ((p3, 0), (p4a, per_z), (p4b, per_z + per_z // 2), (p5, 2 * per_z))
        )
    ]
    for copy in copies + block_copies:
        copy.start()
    e_out[...] = e_in[...]
    slice_out[...] = slice_in[...]
    table[...] = table_in[...]
    for copy in copies:
        copy.wait()
    multiply(hid_v, block_v, block_copies, acc, c, y)
    mine = columns(hid_v, y, width)
    for i in range(3):
        part = slice(i * per_z, (i + 1) * per_z)
        here = pl.ds(pl.multiple_of(lax.rem(z + 3 + i, NZ) * per_z, 64), per_z)
        slice_out[here] = mine[part]
        e_out[here], table[here] = soften(acc[part], targets[here], z, y, x)
    flat = table[...].T
    packed = pack([flat[0:1], flat[1:2], flat[2:3]])
    for i in range(stats_out.shape[0]):
        stats_out[i] = packed


def columns(hid_v, origin, width):
    return hid_v[:, pl.ds(pl.multiple_of(origin * width, 128), width)]


def multiply(hid_v, block_v, block_copies, acc, c, y):
    width = block_v.shape[1]
    for i in range(4):
        core = c if i < 2 else 1 - c
        block_copies[i].wait()
        mine = columns(hid_v, 2 * core + lax.rem(y + i, 2), width)
        term = jnp.dot(mine, block_v[i], preferred_element_type=F32)
        acc[...] = term if i == 0 else acc[...] + term


def soften(logits, targets, z, y, x):
    rows, group = logits.shape
    top = jnp.max(logits, axis=1, keepdims=True)
    e = jnp.exp(logits - top)
    total = jnp.sum(e, axis=1, keepdims=True)
    first = ((z * NC + y // 2) * NX + x) * (2 * group) + lax.rem(y, 2) * group
    ids = first + lax.broadcasted_iota(jnp.int32, (rows, group), 1)
    picked = jnp.sum(jnp.where(ids == targets, logits, 0.0), axis=1, keepdims=True)
    lane = lax.broadcasted_iota(jnp.int32, (rows, 128), 1)
    table = jnp.where(lane == 0, top, jnp.where(lane == 1, total, jnp.where(lane == 2, picked, 0.0)))
    return e.astype(BF16), table


def pack(vectors):
    parts = [v[:, i : i + 128] for v in vectors for i in range(0, v.shape[1], 128)]
    return jnp.concatenate(parts + [jnp.zeros((16 - len(parts), 128), F32)], axis=0)


def unpack(tiles):
    return jnp.concatenate([tiles[i : i + 1] for i in range(tiles.shape[0])], axis=1)


def merged(table):
    m, s, p = table[:, 0:4], table[:, 4:8], table[:, 8:12]
    top = jnp.max(m, axis=0)
    return top, jnp.sum(s * jnp.exp(m - top[None]), axis=0), jnp.sum(p, axis=0)


def wide_kernel(pos, got, out):
    z, x = pos[0], pos[3]
    m, s, p = merged(got[...])
    out[...] = jnp.concatenate([m, s, p, got[z * NX + x][0:4]], axis=0)


def total_kernel(pos, t0, t1, t2, t3, weights, vec_out, log_prob_out):
    tables = [t[...] for t in (t0, t1, t2, t3)]
    m, s, p = (unpack(v) for v in merged(jnp.stack(tables)))
    log_total = m + jnp.log(s)
    log_prob = p - log_total
    w = weights[...]
    rows = [-w * jnp.exp(unpack(t[12:16]) - log_total) for t in tables]
    rows.append(w * (1.0 - jnp.exp(log_prob)))
    rows.append(jnp.zeros((3, m.shape[1]), F32))
    vec_out[...] = jnp.concatenate(rows, axis=0)
    log_prob_out[...] = jnp.broadcast_to(log_prob, log_prob_out.shape)


def grad_kernel(pos, targets, vec, e0, e1, e2, e2b, e3, own, other, g0, g1, keep, s1, s2, s3, part):
    z, c, y, x = (pos[i] for i in range(4))
    rows, group = e0.shape
    cols = jnp.concatenate([vec[...], jnp.zeros((120, rows), F32)], axis=0).T
    t = targets[...]
    opposite = jnp.concatenate([e2[...], e2b[...]], axis=0)
    for d, e in enumerate((e0[...], e1[...], opposite, e3[...])):
        g = lax.rem(y + NY - d, NY)
        first = ((z * NC + g // 2) * NX + x) * (2 * group) + lax.rem(g, 2) * group
        ids = first + lax.broadcasted_iota(jnp.int32, (rows, group), 1)
        value = jnp.where(ids == t, cols[:, 4:5], e.astype(F32) * cols[:, d : d + 1])
        value = value.astype(BF16)
        at = pl.ds(pl.multiple_of(lax.rem(g, 2) * group, 128), group)
        same = g // 2 == c

        @pl.when(same)
        def _():
            g0[:, at] = value

        @pl.when(jnp.logical_not(same))
        def _():
            g1[:, at] = value

    nt = (((1,), (1,)), ((), ()))
    sums = lax.dot_general(g0[...], own[...], nt, preferred_element_type=F32)
    sums += lax.dot_general(g1[...], other[...], nt, preferred_element_type=F32)
    part[...] = sums.reshape(part.shape)
    keep[...] = part[:, x]
    for d, out in enumerate((s1, s2, s3)):
        out[...] = part[:, lax.rem(x + d + 1, NX)].astype(BF16)


def head_kernel(pos, h0, h1, g0, g1, out):
    tn = (((0,), (0,)), ((), ()))
    step = 256
    for i in range(0, out.shape[0], step):
        total = lax.dot_general(h0[:, i : i + step], g0[...], tn, preferred_element_type=F32)
        total += lax.dot_general(h1[:, i : i + step], g1[...], tn, preferred_element_type=F32)
        out[i : i + step] = total.astype(BF16)


def tie(*arrays):
    return lax.optimization_barrier(arrays)


def body(hidden, head, targets, weights):
    rows, width = hidden.shape
    columns = head.shape[1]
    group = columns // 2
    half = width // 2
    per_z = NX * rows
    z, c, y, x = (lax.axis_index(a) for a in ("z", "core", "y", "x"))
    pos = jnp.stack([z, c, y, x]).astype(jnp.int32)

    def copies(v, n, axis):
        flat = jnp.broadcast_to(v[None], (n,) + v.shape).reshape((n * v.shape[0],) + v.shape[1:])
        return lax.all_to_all(flat, axis, 0, 0, tiled=True).reshape((n,) + v.shape)

    near = copies(hidden, NY, "y")

    def block(k):
        return lax.dynamic_slice_in_dim(head, ((y + k) % 2) * group, group, 1)

    def hand_over(v, k):
        perm = [
            (i * NY + j, (j // 2) * NY + 2 * i + (j + k) % 2) for i in range(NC) for j in range(NY)
        ]
        return lax.ppermute(v, ("core", "y"), perm)

    near, block0, block1 = tie(near, block(0), block(1))
    got0, got1 = hand_over(block0, 0), hand_over(block1, 1)
    near = near.transpose(1, 0, 2).reshape(rows, NY * width)
    near = copies(near, NX, "x").reshape(per_z, NY * width)

    def ordered(v):
        v = lax.dynamic_index_in_dim(v.reshape(NZ, NC, per_z), c, 1, False)
        return v.reshape(NZ * per_z)

    my_targets, my_weights = ordered(targets)[:, None], ordered(weights)[None]

    size = NZ * per_z
    def scratch(rows, pieces):
        return [
            pltpu.VMEM((rows, group), F32),
            pltpu.VMEM((rows, NY * width), BF16),
            pltpu.VMEM((NY, width, group), BF16),
            pltpu.SemaphoreType.DMA((pieces,)),
            pltpu.SemaphoreType.DMA((NY,)),
        ]

    pieces, flying = {0: near}, {1: near, -1: near}
    for step in range(1, 5):
        if step == 3:
            got0, got1, head_later, pos, my_targets, my_weights, *tied = tie(
                got0, got1, head, pos, my_targets, my_weights, flying[1], flying[-1]
            )
            flying = {1: tied[0], -1: tied[1]}
            twin0, twin1 = lax.ppermute(got0, "core", SWAP), lax.ppermute(got1, "core", SWAP)
            other = lax.ppermute(head_later, "core", SWAP)
        if step == 4:
            blocks = (got0, got1, twin0, twin1)
            hid = [pieces[r] for r in (0, 1, 2, 6, 7)]
            e, table, mine = call(
                functools.partial(early_kernel, len(hid)),
                [((size, group), BF16), ((size, 128), F32), ((size, width), BF16)],
                (pos, my_targets, *hid, *blocks),
                scratch=scratch(size, len(hid)),
                far=len(hid) + 4,
                vmem=60,
                flops=2 * size * NY * width * group,
                moved=10 * 2**20,
            )
            e, table, mine, *tied = tie(e, table, mine, flying[1], flying[-1])
            flying = {1: tied[0], -1: tied[1]}
            flying = {1: flying[1][: per_z // 2], -1: flying[-1][per_z // 2 :]}
        for d in (1, -1):
            flying[d] = lax.ppermute(flying[d], "z", shift(NZ, d))
            pieces[-d * step if step == 4 else (-d * step) % NZ] = flying[d]

    e, mine, stats = call(
        late_kernel,
        [((size, group), BF16), ((size, width), BF16), ((NZ * NX, 16, 128), F32)],
        (pos, my_targets, e, table, mine, *[pieces[r] for r in (3, 5, -4, 4)], *blocks),
        scratch=[pltpu.VMEM((size, 128), F32)] + scratch(3 * per_z, 4),
        far=8,
        vmem=56,
    )

    e1, e3 = lax.ppermute(e, "y", shift(NY, 1)), lax.ppermute(e, "y", shift(NY, -1))
    far = lax.all_to_all(stats, ("z", "x"), 0, 0, tiled=True)
    e2 = lax.ppermute(e1[: size // 2], "y", shift(NY, 1))
    e2b = lax.ppermute(e3[size // 2 :], "y", shift(NY, -1))
    (wide,) = call(wide_kernel, [((16, 128), F32)], (pos, far))
    tables = [wide] + [lax.ppermute(wide, "y", shift(NY, d)) for d in (1, 2, 3)]
    vec, lp = call(total_kernel, [((8, size), F32), ((8, size), F32)], (pos, *tables, my_weights))
    twin_mine = lax.ppermute(mine, "core", SWAP)
    exps = (e, e1, e2, e2b, e3)

    kept, sent, keep, *send = call(
        grad_kernel,
        [((size, columns), BF16)] * 2
        + [((NZ, rows, width), F32)]
        + [((NZ, rows, width), BF16)] * 3,
        (pos, my_targets, vec, *exps, head, other),
        scratch=[pltpu.VMEM((NZ, NX, rows, width), F32)],
    )
    terms = [lax.ppermute(v, "x", shift(NX, d + 1)) for d, v in enumerate(send)]
    twin_kept = lax.ppermute(sent, "core", SWAP)
    (head_grad,) = call(
        head_kernel,
        [((width, columns), BF16)],
        (pos, mine, twin_mine, kept, twin_kept),
        flops=2 * NZ * NC * per_z * columns * width,
        moved=8 * 2**20,
    )
    head_grad, *terms = tie(head_grad, *terms)

    for term in terms:
        keep = keep + term.astype(F32)
    total = keep.astype(BF16).reshape(NZ * rows, width)
    got = lax.all_to_all(total, "z", 0, 0, tiled=True)
    hidden_grad = jnp.sum(got.reshape(NZ, rows, width).astype(F32), axis=0).astype(BF16)

    log_prob = lp[0]
    own = lax.dynamic_slice_in_dim(log_prob, 2 * y * per_z, 2 * per_z, 0)
    oth = lax.ppermute(own, "core", SWAP)
    pairs = jnp.where(c == 0, jnp.stack([own, oth]), jnp.stack([oth, own]))
    log_prob_out = pairs.reshape(NC, 2, per_z).transpose(1, 0, 2).reshape(-1)
    return log_prob_out, hidden_grad, head_grad


def solution(mesh):
    fine = Mesh(mesh.devices.reshape(NZ, NC, NY, NX), ("z", "core", "y", "x"))
    tok = ("z", "core", "x")
    return jax.shard_map(
        body,
        mesh=fine,
        in_specs=(P(tok, "y"), P("y", tok), P(), P()),
        out_specs=(P("y"), P(tok, "y"), P("y", tok)),
        check_vma=False,
    )
```

```python
import functools

import jax
import jax.numpy as jnp
from jax import lax
from jax.experimental import pallas as pl
from jax.experimental.pallas import tpu as pltpu
from jax.sharding import Mesh, PartitionSpec as P

F32 = jnp.float32
BF16 = jnp.bfloat16
NZ, NC, NY, NX = 8, 2, 4, 4
VMEM = pl.BlockSpec(memory_space=pltpu.VMEM)
SMEM = pl.BlockSpec(memory_space=pltpu.SMEM)


def shift(n, d):
    return [(i, (i + d) % n) for i in range(n)]


SWAP = [(0, 1), (1, 0)]


ANY = pl.BlockSpec(memory_space=pl.ANY)


def call(kernel, outs, args, scratch=(), flops=1000, moved=1000, far=0, vmem=24):
    return pl.pallas_call(
        kernel,
        out_shape=[jax.ShapeDtypeStruct(s, d) for s, d in outs],
        in_specs=[SMEM] + [VMEM] * (len(args) - 1 - far) + [ANY] * far,
        out_specs=[VMEM] * len(outs),
        scratch_shapes=list(scratch),
        cost_estimate=pl.CostEstimate(flops=flops, bytes_accessed=moved, transcendentals=0),
        compiler_params=pltpu.CompilerParams(vmem_limit_bytes=vmem * 2**20),
    )(*args)


def rows_kernel(aheads, count, first, last, pos, targets, *refs):
    refs = list(refs)
    before = [] if first else [refs.pop(0) for _ in range(3)]
    pieces, blocks = refs[:count], refs[count : count + 4]
    e_out, slice_out, third = refs[count + 4 : count + 7]
    rest = refs[count + 7 :]
    table = rest.pop(0) if last else third
    acc, hid_v, block_v, hid_sem, block_sem = rest
    z, c, y, x = (pos[i] for i in range(4))
    width = block_v.shape[1]
    per_z, size = hid_v.shape[0] // len(aheads), hid_v.shape[0] // count
    copies = [
        pltpu.make_async_copy(p, hid_v.at[pl.ds(i * size, size)], hid_sem.at[i])
        for i, p in enumerate(pieces)
    ]
    block_copies = [
        pltpu.make_async_copy(b, block_v.at[i], block_sem.at[i]) for i, b in enumerate(blocks)
    ]
    for copy in copies + block_copies:
        copy.start()
    for old, new in zip(before, (e_out, slice_out, table)):
        new[...] = old[...]
    for copy in copies:
        copy.wait()
    multiply(hid_v, block_v, block_copies, acc, c, y)
    mine = columns(hid_v, y, width)
    for i, ahead in enumerate(aheads):
        part = slice(i * per_z, (i + 1) * per_z)
        here = pl.ds(pl.multiple_of(lax.rem(z + ahead, NZ) * per_z, 64), per_z)
        slice_out[here] = mine[part]
        e_out[here], table[here] = soften(acc[part], targets[here], z, y, x)
    if last:
        flat = table[...].T
        packed = pack([flat[0:1], flat[1:2], flat[2:3]])
        for i in range(third.shape[0]):
            third[i] = packed


def columns(hid_v, origin, width):
    return hid_v[:, pl.ds(pl.multiple_of(origin * width, 128), width)]


def multiply(hid_v, block_v, block_copies, acc, c, y):
    width = block_v.shape[1]
    for i in range(4):
        core = c if i < 2 else 1 - c
        block_copies[i].wait()
        mine = columns(hid_v, 2 * core + lax.rem(y + i, 2), width)
        term = jnp.dot(mine, block_v[i], preferred_element_type=F32)
        acc[...] = term if i == 0 else acc[...] + term


def soften(logits, targets, z, y, x):
    rows, group = logits.shape
    top = jnp.max(logits, axis=1, keepdims=True)
    e = jnp.exp(logits - top)
    total = jnp.sum(e, axis=1, keepdims=True)
    first = ((z * NC + y // 2) * NX + x) * (2 * group) + lax.rem(y, 2) * group
    ids = first + lax.broadcasted_iota(jnp.int32, (rows, group), 1)
    picked = jnp.sum(jnp.where(ids == targets, logits, 0.0), axis=1, keepdims=True)
    lane = lax.broadcasted_iota(jnp.int32, (rows, 128), 1)
    table = jnp.where(lane == 0, top, jnp.where(lane == 1, total, jnp.where(lane == 2, picked, 0.0)))
    return e.astype(BF16), table


def pack(vectors):
    parts = [v[:, i : i + 128] for v in vectors for i in range(0, v.shape[1], 128)]
    return jnp.concatenate(parts + [jnp.zeros((16 - len(parts), 128), F32)], axis=0)


def unpack(tiles):
    return jnp.concatenate([tiles[i : i + 1] for i in range(tiles.shape[0])], axis=1)


def merged(table):
    m, s, p = table[:, 0:4], table[:, 4:8], table[:, 8:12]
    top = jnp.max(m, axis=0)
    return top, jnp.sum(s * jnp.exp(m - top[None]), axis=0), jnp.sum(p, axis=0)


def wide_kernel(pos, got, out):
    z, x = pos[0], pos[3]
    m, s, p = merged(got[...])
    out[...] = jnp.concatenate([m, s, p, got[z * NX + x][0:4]], axis=0)


def total_kernel(pos, t0, t1, t2, t3, weights, vec_out, log_prob_out):
    tables = [t[...] for t in (t0, t1, t2, t3)]
    m, s, p = (unpack(v) for v in merged(jnp.stack(tables)))
    log_total = m + jnp.log(s)
    log_prob = p - log_total
    w = weights[...]
    rows = [-w * jnp.exp(unpack(t[12:16]) - log_total) for t in tables]
    rows.append(w * (1.0 - jnp.exp(log_prob)))
    rows.append(jnp.zeros((3, m.shape[1]), F32))
    vec_out[...] = jnp.concatenate(rows, axis=0)
    log_prob_out[...] = jnp.broadcast_to(log_prob, log_prob_out.shape)


def grad_kernel(pos, targets, vec, e0, e1, e2, e2b, e3, own, other, g0, g1, keep, s1, s2, s3, part):
    z, c, y, x = (pos[i] for i in range(4))
    rows, group = e0.shape
    cols = jnp.concatenate([vec[...], jnp.zeros((120, rows), F32)], axis=0).T
    t = targets[...]
    opposite = jnp.concatenate([e2[...], e2b[...]], axis=0)
    for d, e in enumerate((e0[...], e1[...], opposite, e3[...])):
        g = lax.rem(y + NY - d, NY)
        first = ((z * NC + g // 2) * NX + x) * (2 * group) + lax.rem(g, 2) * group
        ids = first + lax.broadcasted_iota(jnp.int32, (rows, group), 1)
        value = jnp.where(ids == t, cols[:, 4:5], e.astype(F32) * cols[:, d : d + 1])
        value = value.astype(BF16)
        at = pl.ds(pl.multiple_of(lax.rem(g, 2) * group, 128), group)
        same = g // 2 == c

        @pl.when(same)
        def _():
            g0[:, at] = value

        @pl.when(jnp.logical_not(same))
        def _():
            g1[:, at] = value

    nt = (((1,), (1,)), ((), ()))
    sums = lax.dot_general(g0[...], own[...], nt, preferred_element_type=F32)
    sums += lax.dot_general(g1[...], other[...], nt, preferred_element_type=F32)
    part[...] = sums.reshape(part.shape)
    keep[...] = part[:, x]
    for d, out in enumerate((s1, s2, s3)):
        out[...] = part[:, lax.rem(x + d + 1, NX)].astype(BF16)


def head_kernel(pos, h0, h1, g0, g1, out):
    tn = (((0,), (0,)), ((), ()))
    step = 256
    for i in range(0, out.shape[0], step):
        total = lax.dot_general(h0[:, i : i + step], g0[...], tn, preferred_element_type=F32)
        total += lax.dot_general(h1[:, i : i + step], g1[...], tn, preferred_element_type=F32)
        out[i : i + step] = total.astype(BF16)


def tie(*arrays):
    return lax.optimization_barrier(arrays)


def body(hidden, head, targets, weights):
    rows, width = hidden.shape
    columns = head.shape[1]
    group = columns // 2
    half = width // 2
    per_z = NX * rows
    z, c, y, x = (lax.axis_index(a) for a in ("z", "core", "y", "x"))
    pos = jnp.stack([z, c, y, x]).astype(jnp.int32)

    def copies(v, n, axis):
        flat = jnp.broadcast_to(v[None], (n,) + v.shape).reshape((n * v.shape[0],) + v.shape[1:])
        return lax.all_to_all(flat, axis, 0, 0, tiled=True).reshape((n,) + v.shape)

    near = copies(hidden, NY, "y")

    def block(k):
        return lax.dynamic_slice_in_dim(head, ((y + k) % 2) * group, group, 1)

    def hand_over(v, k):
        perm = [
            (i * NY + j, (j // 2) * NY + 2 * i + (j + k) % 2) for i in range(NC) for j in range(NY)
        ]
        return lax.ppermute(v, ("core", "y"), perm)

    near, block0, block1 = tie(near, block(0), block(1))
    got0, got1 = hand_over(block0, 0), hand_over(block1, 1)
    near = near.transpose(1, 0, 2).reshape(rows, NY * width)
    near = copies(near, NX, "x").reshape(per_z, NY * width)

    def ordered(v):
        v = lax.dynamic_index_in_dim(v.reshape(NZ, NC, per_z), c, 1, False)
        return v.reshape(NZ * per_z)

    my_targets, my_weights = ordered(targets)[:, None], ordered(weights)[None]

    size = NZ * per_z
    def logits_stage(aheads, pieces, before=(), last=False):
        count, held = len(pieces), len(aheads) * per_z
        third = ((NZ * NX, 16, 128), F32) if last else ((size, 128), F32)
        return call(
            functools.partial(rows_kernel, aheads, count, not before, last),
            [((size, group), BF16), ((size, width), BF16), third],
            (pos, my_targets, *before, *pieces, *blocks),
            scratch=[pltpu.VMEM((size, 128), F32)] * last
            + [
                pltpu.VMEM((held, group), F32),
                pltpu.VMEM((held, NY * width), BF16),
                pltpu.VMEM((NY, width, group), BF16),
                pltpu.SemaphoreType.DMA((count,)),
                pltpu.SemaphoreType.DMA((NY,)),
            ],
            far=count + 4,
            vmem=56 if before else 60,
            flops=1000 if last else 2 * size * NY * width * group,
            moved=1000 if last else 10 * 2**20,
        )

    pieces, flying = {0: near}, {1: near, -1: near}
    for step in range(1, 5):
        if step == 3:
            got0, got1, head_later, pos, my_targets, my_weights, *tied = tie(
                got0, got1, head, pos, my_targets, my_weights, flying[1], flying[-1]
            )
            flying = {1: tied[0], -1: tied[1]}
            twin0, twin1 = lax.ppermute(got0, "core", SWAP), lax.ppermute(got1, "core", SWAP)
            other = lax.ppermute(head_later, "core", SWAP)
        if step == 4:
            blocks = (got0, got1, twin0, twin1)
            e, mine, table = logits_stage((0, 1, 2, 6, 7), [pieces[r] for r in (0, 1, 2, 6, 7)])
            e, table, mine, *tied = tie(e, table, mine, flying[1], flying[-1])
            flying = {1: tied[0], -1: tied[1]}
            flying = {1: flying[1][: per_z // 2], -1: flying[-1][per_z // 2 :]}
        for d in (1, -1):
            flying[d] = lax.ppermute(flying[d], "z", shift(NZ, d))
            pieces[-d * step if step == 4 else (-d * step) % NZ] = flying[d]

    e, mine, table = logits_stage((3, 5), [pieces[3], pieces[5]], (e, mine, table))
    e, mine, stats = logits_stage((4,), [pieces[-4], pieces[4]], (e, mine, table), last=True)

    e1, e3 = lax.ppermute(e, "y", shift(NY, 1)), lax.ppermute(e, "y", shift(NY, -1))
    far = lax.all_to_all(stats, ("z", "x"), 0, 0, tiled=True)
    e2 = lax.ppermute(e1[: size // 2], "y", shift(NY, 1))
    e2b = lax.ppermute(e3[size // 2 :], "y", shift(NY, -1))
    (wide,) = call(wide_kernel, [((16, 128), F32)], (pos, far))
    tables = [wide] + [lax.ppermute(wide, "y", shift(NY, d)) for d in (1, 2, 3)]
    vec, lp = call(total_kernel, [((8, size), F32), ((8, size), F32)], (pos, *tables, my_weights))
    twin_mine = lax.ppermute(mine, "core", SWAP)
    exps = (e, e1, e2, e2b, e3)

    kept, sent, keep, *send = call(
        grad_kernel,
        [((size, columns), BF16)] * 2
        + [((NZ, rows, width), F32)]
        + [((NZ, rows, width), BF16)] * 3,
        (pos, my_targets, vec, *exps, head, other),
        scratch=[pltpu.VMEM((NZ, NX, rows, width), F32)],
    )
    terms = [lax.ppermute(v, "x", shift(NX, d + 1)) for d, v in enumerate(send)]
    twin_kept = lax.ppermute(sent, "core", SWAP)
    (head_grad,) = call(
        head_kernel,
        [((width, columns), BF16)],
        (pos, mine, twin_mine, kept, twin_kept),
        flops=2 * NZ * NC * per_z * columns * width,
        moved=8 * 2**20,
    )
    head_grad, *terms = tie(head_grad, *terms)

    for term in terms:
        keep = keep + term.astype(F32)
    total = keep.astype(BF16).reshape(NZ * rows, width)
    got = lax.all_to_all(total, "z", 0, 0, tiled=True)
    hidden_grad = jnp.sum(got.reshape(NZ, rows, width).astype(F32), axis=0).astype(BF16)

    log_prob = lp[0]
    own = lax.dynamic_slice_in_dim(log_prob, 2 * y * per_z, 2 * per_z, 0)
    oth = lax.ppermute(own, "core", SWAP)
    pairs = jnp.where(c == 0, jnp.stack([own, oth]), jnp.stack([oth, own]))
    log_prob_out = pairs.reshape(NC, 2, per_z).transpose(1, 0, 2).reshape(-1)
    return log_prob_out, hidden_grad, head_grad


def solution(mesh):
    fine = Mesh(mesh.devices.reshape(NZ, NC, NY, NX), ("z", "core", "y", "x"))
    tok = ("z", "core", "x")
    return jax.shard_map(
        body,
        mesh=fine,
        in_specs=(P(tok, "y"), P("y", tok), P(), P()),
        out_specs=(P("y"), P(tok, "y"), P("y", tok)),
        check_vma=False,
    )
```
